32 devices in a mesh: src: 8 (over z, y), rcv: 4 (over x, core).
Axes of the slice: x: 2, y: 2, z: 4, core: 2. Of those that a mesh axis runs over, the one named last changes fastest.
Arguments:
- field: bfloat16 [2, 8192, 1024], P(None, 'rcv', 'src'), may hold values from -6 to 6
- u_basis: bfloat16 [8, 4, 2, 8, 2, 160, 256], P('src', 'rcv'), may hold values from -0.0625 to 0.0625
- v_basis: bfloat16 [8, 4, 2, 8, 160, 2, 256], P('src', 'rcv'), may hold values from -0.25 to 0.25
- tile_ranks: int32 [8, 4, 2, 8], P('src', 'rcv'), may hold values from 32 to 160, as said below
- window_start: int32 [8], replicated, may hold values from 0 to 8
Outputs:
- predicted: bfloat16 [2, 2048, 1024], P(None, 'rcv', 'src')
The draws below stay inside these ranges and needn't reach their ends.
Inputs may be any that keep to these rules, and one draw needn't show every extreme that they name: `tile_ranks`: on every device of the mesh at least one of its tiles has rank 160.
All inputs are finite; a program needn't handle non-finite values.
Results may differ from the reference program's by a relative error of at most 0.0058.
Values may be sent and summed in bfloat16 or wider, within the bound.
No kernel may reach another device: no remote copies, remote signals or barrier semaphores. Data moves between devices by JAX's collectives and lax.ppermute only.
A program may use at most 192 MiB of HBM per device.

```python
import jax
import jax.numpy as jnp
from jax import lax

B = 256
RMAX = 160
RMIN = 32
JT = 8
MTD = 2
AR = 8
CD = 128
NT = 32
MT = 16
N = 8192
C = 1024
N_SRC = 8
N_RCV = 4


def draw_tile_ranks(key, part):
    first_key, second_key = jax.random.split(jax.random.fold_in(key, 17))
    base_ranks = jax.random.randint(first_key, (N_SRC, N_RCV, MTD * JT), RMIN, RMAX + 1, dtype=jnp.int32)
    chosen_spot = jax.random.randint(second_key, (N_SRC, N_RCV), 0, MTD * JT, dtype=jnp.int32)
    spot_hit = jnp.arange(MTD * JT, dtype=jnp.int32)[None, None, :] == chosen_spot[:, :, None]
    full_ranks = jnp.where(spot_hit, jnp.int32(RMAX), base_ranks)
    return full_ranks.reshape(N_SRC, N_RCV, MTD, JT)


def with_ends(values, stream_key, low, largest):
    place = [jax.random.randint(jax.random.fold_in(stream_key, axis), (), 0, length) for axis, length in enumerate(values.shape)]
    main_axis = values.shape.index(max(values.shape))
    beside = place[:main_axis] + [(place[main_axis] + 1) % values.shape[main_axis]] + place[main_axis + 1:]
    return values.at[tuple(place)].set(low).at[tuple(beside)].set(largest)


def block_scale(own_key, extent, pieces, smallest, high):
    loudness = 1.0
    for dim, parts in pieces:
        steps = jax.random.uniform(jax.random.fold_in(jax.random.fold_in(own_key, 6), dim), (parts,), jnp.float32, smallest / len(pieces), high / len(pieces))
        loudness = loudness * jnp.repeat(jnp.exp(steps), extent[dim] // parts).reshape((-1,) + (1,) * (len(extent) - 1 - dim))
    return loudness


def gaussian(key, dims, width, reach, cuts=(), kind=jnp.bfloat16):
    result = width * jax.random.normal(key, dims, jnp.float32)
    if cuts:
        result = result * block_scale(key, dims, cuts, -0.22, 0.18)
    return jnp.clip(result, -reach, reach).astype(kind)


def setup_inputs(seed: int = 0) -> dict:
    streams_of = jax.random.split(jax.random.key(seed), 6)
    return {
        "field": gaussian(streams_of[0], (2, N, C), 1.0, 6.0, ((1, 4), (2, 8))),
        "u_basis": gaussian(streams_of[1], (N_SRC, N_RCV, MTD, JT, 2, RMAX, B), (2 * RMAX * NT) ** -0.5, 0.0625, ((0, 8), (1, 4))),
        "v_basis": gaussian(streams_of[2], (N_SRC, N_RCV, MTD, JT, RMAX, 2, B), (2 * B) ** -0.5, 0.25, ((0, 8), (1, 4))),
        "tile_ranks": draw_tile_ranks(jax.random.fold_in(streams_of[5], 71), 0),
        "window_start": with_ends(jax.random.randint(streams_of[4], (N_SRC,), 0, MT - AR + 1), jax.random.fold_in(streams_of[4], 1), 0, MT - AR).astype(jnp.int32),
    }


def expand_block(field_block):
    real_part = field_block[0]
    imag_part = field_block[1]
    upper = jnp.concatenate([real_part, imag_part], axis=1)
    lower = jnp.concatenate([imag_part, -real_part], axis=1)
    return jnp.concatenate([upper, lower], axis=0)


def tile_products(u_tiles, v_tiles, rank_list, expanded):
    n_items = v_tiles.shape[0]
    rank_most = v_tiles.shape[1]
    flat_v = v_tiles.reshape(n_items, rank_most, -1).astype(jnp.float32)
    projected = jnp.einsum('nkq,qc->nkc', flat_v, expanded.astype(jnp.float32))
    rank_keep = jnp.arange(rank_most, dtype=jnp.int32)[None, :] < rank_list[:, None]
    projected = jnp.where(rank_keep[:, :, None], projected, jnp.float32(0.0)).astype(jnp.bfloat16)
    half_cols = projected.shape[2] // 2
    w_real = projected[:, :, :half_cols]
    w_imag = projected[:, :, half_cols:]
    stacked = jnp.concatenate([projected, jnp.concatenate([-w_imag, w_real], axis=2)], axis=1)
    flat_u = u_tiles.reshape(n_items, 2 * rank_most, -1).astype(jnp.float32)
    return jnp.einsum('nkp,nkc->npc', flat_u, stacked.astype(jnp.float32))


def reference(field, u_basis, v_basis, tile_ranks, window_start):
    spacing = N_SRC // JT
    steps_t = jnp.arange(AR, dtype=jnp.int32)

    def one_reader(reader):
        first_row = window_start[reader]
        row_ids = first_row + steps_t
        columns = lax.dynamic_slice_in_dim(field, reader * CD, CD, 2)

        def add_column(running, col):
            col_group = col // JT
            col_local = col % JT
            field_block = lax.dynamic_slice_in_dim(columns, col * B, B, 1)
            expanded = expand_block(field_block)
            owners = ((row_ids + spacing * col_local) % N_SRC).astype(jnp.int32)
            levels = (row_ids // N_SRC).astype(jnp.int32)
            u_tiles = u_basis[owners, col_group, levels, col_local]
            v_tiles = v_basis[owners, col_group, levels, col_local]
            rank_list = tile_ranks[owners, col_group, levels, col_local]
            term = tile_products(u_tiles, v_tiles, rank_list, expanded).astype(jnp.bfloat16)
            term = lax.optimization_barrier(term)
            return running + term.astype(jnp.float32), None

        start_sum = jnp.zeros((AR, B, 2 * CD), jnp.float32)
        running, unused = lax.scan(add_column, start_sum, jnp.arange(NT, dtype=jnp.int32))
        return running

    reader_parts = lax.map(one_reader, jnp.arange(N_SRC, dtype=jnp.int32))
    arranged = reader_parts.reshape(N_SRC, AR * B, 2, CD).transpose(2, 1, 0, 3)
    return arranged.reshape(2, AR * B, N_SRC * CD).astype(jnp.bfloat16)
```

```python
import functools

import jax
import jax.numpy as jnp
from jax import lax
from jax.experimental import pallas as pl
from jax.experimental.pallas import tpu as pltpu
from jax.sharding import PartitionSpec as P

AR = 8


def apply_tiles(u_rows, v_rows, expanded):
    n_items = v_rows.shape[0]
    rank_most = v_rows.shape[1]
    flat_v = v_rows.reshape(n_items, rank_most, -1)
    projected = lax.dot_general(
        flat_v, expanded, (((2,), (1,)), ((0,), (0,))), preferred_element_type=jnp.float32
    )
    projected = projected.astype(jnp.bfloat16)
    half_cols = projected.shape[2] // 2
    w_real = projected[:, :, :half_cols]
    w_imag = projected[:, :, half_cols:]
    stacked = jnp.concatenate([projected, jnp.concatenate([-w_imag, w_real], axis=2)], axis=1)
    flat_u = u_rows.reshape(n_items, 2 * rank_most, -1)
    result = lax.dot_general(
        flat_u, stacked, (((1,), (1,)), ((0,), (0,))), preferred_element_type=jnp.float32
    )
    return result.astype(jnp.bfloat16)


def widen_blocks(real_part, imag_part):
    upper = jnp.concatenate([real_part, imag_part], axis=2)
    lower = jnp.concatenate([imag_part, -real_part], axis=2)
    return jnp.concatenate([upper, lower], axis=1)


def general_body(field, u_basis, v_basis, tile_ranks, window_start):
    n_src = lax.axis_size("src")
    levels = u_basis.shape[2]
    col_tiles = u_basis.shape[3]
    rank_most = u_basis.shape[5]
    tile_size = u_basis.shape[6]
    columns = field.shape[2]
    spacing = n_src // col_tiles
    capacity = AR // spacing
    holder = lax.axis_index("src")
    local_u = u_basis.reshape(levels * col_tiles, 2, rank_most, tile_size)
    local_v = v_basis.reshape(levels * col_tiles, rank_most, 2, tile_size)
    rank_list = tile_ranks.reshape(levels * col_tiles)
    rank_keep = jnp.arange(rank_most, dtype=jnp.int32)[None, :] < rank_list[:, None]
    masked_v = jnp.where(rank_keep[:, :, None, None], local_v, jnp.zeros_like(local_v))
    col_ids = jnp.arange(col_tiles, dtype=jnp.int32)
    offsets = (holder - spacing * col_ids[None, :] - window_start[:, None]) % n_src
    inside = offsets < AR
    row_ids = window_start[:, None] + offsets
    tile_ids = row_ids // n_src * col_tiles + col_ids[None, :]
    slot_pos = jnp.cumsum(inside.astype(jnp.int32), axis=1) - 1
    slot_range = jnp.arange(capacity, dtype=jnp.int32)
    slot_match = inside[:, None, :] & (slot_pos[:, None, :] == slot_range[None, :, None])
    picked = jnp.sum(jnp.where(slot_match, tile_ids[:, None, :], 0), axis=2).reshape(-1)
    window_first = window_start[holder]
    t_ids = jnp.arange(AR, dtype=jnp.int32)
    sources = (window_first + t_ids[None, :] + spacing * col_ids[:, None]) % n_src
    earlier = (sources[:, :, None] - spacing * col_ids[None, None, :] - window_first) % n_src < AR
    before = col_ids[None, None, :] < col_ids[:, None, None]
    entries = jnp.sum((earlier & before).astype(jnp.int32), axis=2)
    item_ids = sources * capacity + entries
    blocks = field.reshape(2, col_tiles, tile_size, columns)
    slot_ids = jnp.arange(n_src * capacity, dtype=jnp.int32)
    slot_hit = item_ids[None, :, :] == slot_ids[:, None, None]
    slot_col = jnp.sum(jnp.where(slot_hit, col_ids[None, :, None], 0), axis=(1, 2))
    raw_blocks = jnp.swapaxes(blocks, 0, 1)
    send_f = jnp.take(raw_blocks, slot_col, axis=0)
    got_f = lax.all_to_all(send_f, "src", split_axis=0, concat_axis=0, tiled=True)
    widened = widen_blocks(got_f[:, 0], got_f[:, 1])
    own_u = jnp.take(local_u, picked, axis=0)
    own_v = jnp.take(masked_v, picked, axis=0)
    tile_out = apply_tiles(own_u, own_v, widened)
    returned = lax.all_to_all(tile_out, "src", split_axis=0, concat_axis=0, tiled=True)
    ordering = jnp.transpose(item_ids).reshape(-1)
    gathered = jnp.take(returned, ordering, axis=0).reshape(AR, col_tiles, tile_size, 2 * columns)
    accum = jnp.sum(gathered.astype(jnp.float32), axis=1)
    flat_rows = accum.reshape(AR * tile_size, 2 * columns)
    summed = lax.psum(flat_rows, "rcv")
    share = flat_rows.shape[0] // lax.axis_size("rcv")
    own_rows = lax.dynamic_slice_in_dim(summed, lax.axis_index("rcv") * share, share, 0)
    rounded = own_rows.astype(jnp.bfloat16)
    return rounded.reshape(-1, 2, columns).transpose(1, 0, 2)


def dot(a, b, ca=1):
    return lax.dot_general(a, b, (((ca,), (0,)), ((), ())), preferred_element_type=jnp.float32)


def tile_term(f, v, u):
    f_real, f_imag = f[0, 0], f[1, 0]
    n = f_real.shape[1]
    w = dot(v[0, 0, 0], jnp.concatenate([f_real, f_imag], axis=1))
    w += dot(v[0, 0, 1], jnp.concatenate([f_imag, -f_real], axis=1))
    w = w.astype(jnp.bfloat16)
    turned = jnp.concatenate([-w[:, n:], w[:, :n]], axis=1)
    return dot(u[0, 0, 0], w, 0) + dot(u[0, 0, 1], turned, 0)


def stage_kernel(n_readers, steps, meta, va, vb, ua, ub, *rest):
    fields, (send, keep) = rest[: 2 * n_readers], rest[2 * n_readers :]
    reader, step = pl.program_id(0), pl.program_id(1)
    half = send.shape[1]

    def work(fa, fb):
        total = tile_term(fa, va, ua) + tile_term(fb, vb, ub)
        slot = meta[(n_readers + reader) * steps + step]
        place = lax.rem(slot, half)

        @pl.when(slot < half)
        def _():
            send[0, place] = total.astype(jnp.bfloat16)

        @pl.when(slot >= half)
        def _():
            keep[0, place] = total

    for n in range(n_readers):
        if n_readers == 1:
            work(fields[0], fields[1])
        else:
            pl.when(reader == n)(functools.partial(work, fields[2 * n], fields[2 * n + 1]))


def run_stage(levels, slots, tiles, fields):
    va, vb, ua, ub = tiles
    n_readers = len(fields) // 2
    steps, rank_most, size = va.shape[1], va.shape[3], va.shape[4]
    columns = fields[0].shape[-1]
    half = steps // 2
    meta = jnp.concatenate([levels.reshape(-1), slots.reshape(-1)])
    tile_spec = pl.BlockSpec(
        (1, 1, 2, rank_most, size), lambda n, g, m: (m[n * steps + g], g, 0, 0, 0)
    )

    def field_spec(own):
        def index(n, g, m):
            block = g if n_readers == 1 else jnp.where(n == own, g, jnp.where(n < own, 0, steps - 1))
            return (0, block, 0, 0)

        return pl.BlockSpec((2, 1, size, columns), index)

    out_spec = pl.BlockSpec((1, half, size, 2 * columns), lambda n, g, m: (n, 0, 0, 0))
    out_dims = (n_readers, half, size, 2 * columns)
    n_items = n_readers * steps * 2
    return pl.pallas_call(
        functools.partial(stage_kernel, n_readers, steps),
        grid_spec=pltpu.PrefetchScalarGridSpec(
            num_scalar_prefetch=1,
            grid=(n_readers, steps),
            in_specs=[tile_spec] * 4 + [field_spec(n // 2) for n in range(2 * n_readers)],
            out_specs=[out_spec] * 2,
        ),
        out_shape=[
            jax.ShapeDtypeStruct(out_dims, jnp.bfloat16),
            jax.ShapeDtypeStruct(out_dims, jnp.float32),
        ],
        compiler_params=pltpu.CompilerParams(vmem_limit_bytes=32 << 20),
        cost_estimate=pl.CostEstimate(
            flops=n_items * 16 * rank_most * size * columns,
            bytes_accessed=n_items * 8 * rank_most * size + 6 * n_readers * steps * size * columns * 2,
            transcendentals=0,
        ),
        name="tile_stage",
    )(meta, va, vb, ua, ub, *fields)


def gather_kernel(n_parts, parity, *refs):
    parts, total = refs[:n_parts], refs[n_parts]
    total[...] = jnp.zeros_like(total)
    for n in range(n_parts):
        total[parity[n]] += parts[n][0].astype(jnp.float32)


def add_parts(parts, parity):
    half, size, width = parts[0].shape
    return pl.pallas_call(
        functools.partial(gather_kernel, len(parts)),
        grid_spec=pltpu.PrefetchScalarGridSpec(
            num_scalar_prefetch=1,
            grid=(half,),
            in_specs=[pl.BlockSpec((1, size, width), lambda g, m: (g, 0, 0))] * len(parts),
            out_specs=pl.BlockSpec((2, size, width), lambda g, m: (g, 0, 0)),
        ),
        out_shape=jax.ShapeDtypeStruct((2 * half, size, width), jnp.float32),
        compiler_params=pltpu.CompilerParams(vmem_limit_bytes=32 << 20),
        name="add_parts",
    )(parity, *parts)


def ring_body(field, u_basis, v_basis, tile_ranks, window_start):
    n_src = lax.axis_size("src")
    _, _, levels, col_tiles, _, rank_most, size = u_basis.shape
    columns = field.shape[2]
    steps = col_tiles // 2
    half = steps // 2
    ring = list(range(0, n_src, 2)) + list(range(n_src - 1, 0, -2))
    holder = lax.axis_index("src")
    rcv = lax.axis_index("rcv")
    core = rcv % 2
    chip_x = rcv // 2

    def shift(array, by):
        return lax.ppermute(array, "src", [(ring[n], ring[(n + by) % n_src]) for n in range(n_src)])

    def swap_core(array):
        return lax.ppermute(array, "rcv", [(n, n ^ 1) for n in range(lax.axis_size("rcv"))])

    def swap_x(array):
        return lax.ppermute(array, "rcv", [(n, n ^ 2) for n in range(lax.axis_size("rcv"))])

    def pick(array, axis, index):
        return lax.dynamic_index_in_dim(array, index, axis, keepdims=False)

    blocks = field.reshape(2, steps, 2, size, columns)
    field_a = pick(blocks, 2, core)
    field_b = swap_core(pick(blocks, 2, 1 - core))

    from_left = {0: (field_a, field_b)}
    from_right = {0: (field_a, field_b)}
    far = n_src // 2
    for k in range(1, far):
        from_left[k] = tuple(shift(part, 1) for part in from_left[k - 1])
        from_right[k] = tuple(shift(part, -1) for part in from_right[k - 1])
    far_a = shift(from_left[far - 1][0], 1)
    far_b = shift(from_right[far - 1][1], -1)

    keep_rows = jnp.arange(rank_most, dtype=jnp.int32) < tile_ranks[0, 0][:, :, None]
    v_turned = jnp.swapaxes(v_basis[0, 0], 2, 3)
    v_turned = jnp.where(keep_rows[:, :, None, :, None], v_turned, jnp.zeros_like(v_turned))
    v_split = v_turned.reshape(levels, steps, 2, 2, rank_most, size)
    u_split = u_basis[0, 0].reshape(levels, steps, 2, 2, rank_most, size)
    tiles = (
        pick(v_split, 2, core),
        swap_core(pick(v_split, 2, 1 - core)),
        pick(u_split, 2, core),
        swap_core(pick(u_split, 2, 1 - core)),
    )

    ring_ids = jnp.array(ring, jnp.int32)
    place = jnp.argmax(ring_ids == holder).astype(jnp.int32)
    away = [0]
    for k in range(1, far):
        away += [-k, k]
    away += [far]
    readers = ring_ids[(place + jnp.array(away, jnp.int32)) % n_src]
    starts = window_start[readers][:, None]
    cols = 2 * jnp.arange(steps, dtype=jnp.int32)[None, :] + core
    rows = (holder - cols - starts) % n_src
    tile_levels = (starts + rows) // n_src
    other = (rows // steps != chip_x).astype(jnp.int32)
    slots = (rows % steps) // 2 + half * (1 - other)
    parity = (ring_ids[(place - jnp.array(away, jnp.int32)) % n_src] - core - window_start[holder]) % 2

    def stage(first, count, fields):
        send, keep = run_stage(
            tile_levels[first : first + count], slots[first : first + count], tiles, fields
        )
        return (keep + swap_x(send).astype(jnp.float32)).astype(jnp.bfloat16)

    parts = [stage(0, 1, from_left[0])[0]]
    for k in range(1, far):
        both = stage(2 * k - 1, 2, from_left[k] + from_right[k])
        parts += [shift(both[0], -k), shift(both[1], k)]
    parts += [shift(stage(2 * far - 1, 1, (far_a, far_b))[0], far)]

    total = add_parts(parts, parity)
    mine = lax.dynamic_slice_in_dim(total, core * half, half, 0)
    others = lax.dynamic_slice_in_dim(total, (1 - core) * half, half, 0)
    mine = (mine + swap_core(others.astype(jnp.bfloat16)).astype(jnp.float32)).astype(jnp.bfloat16)
    return mine.reshape(half * size, 2, columns).transpose(1, 0, 2)


def solution(mesh):
    n_src, n_rcv = mesh.shape["src"], mesh.shape["rcv"]

    def body(field, u_basis, v_basis, tile_ranks, window_start):
        col_tiles = u_basis.shape[3]
        ring = n_src == col_tiles == AR and n_rcv == 4
        chosen = ring_body if ring else general_body
        return chosen(field, u_basis, v_basis, tile_ranks, window_start)

    return jax.shard_map(
        body,
        mesh=mesh,
        in_specs=(
            P(None, "rcv", "src"),
            P("src", "rcv", None, None, None, None, None),
            P("src", "rcv", None, None, None, None, None),
            P("src", "rcv", None, None),
            P(),
        ),
        out_specs=P(None, "rcv", "src"),
        check_vma=False,
    )
```
